32 devices in a mesh: row: 4 (over z), col: 8 (over y, x, core).
Axes of the slice: x: 2, y: 2, z: 4, core: 2. Of those that a mesh axis runs over, the one named last changes fastest.
Arguments:
- tokens: bfloat16 [64, 8192], P('row', 'col'), may hold values from -6 to 6
- gate_weight: bfloat16 [8192, 26624], P('col', 'row'), may hold values from -0.0625 to 0.0625
- up_weight: bfloat16 [8192, 26624], P('col', 'row'), may hold values from -0.0625 to 0.0625
- down_weight: bfloat16 [26624, 8192], P('row', 'col'), may hold values from -0.0390625 to 0.0390625
- gate_tangent: bfloat16 [8192, 26624], P('col', 'row'), may hold values from -0.0625 to 0.0625
- up_tangent: bfloat16 [8192, 26624], P('col', 'row'), may hold values from -0.0625 to 0.0625
Outputs:
- gate_product: bfloat16 [8192, 26624], P('col', 'row')
- up_product: bfloat16 [8192, 26624], P('col', 'row')
The draws below stay inside these ranges and needn't reach their ends.
All inputs are finite; a program needn't handle non-finite values.
Results may differ from the reference program's by a relative error of at most 0.0085.
Values may be sent and summed in bfloat16 or wider, within the bound.
A program may use at most 192 MiB of HBM per device.

```python
import jax
import jax.numpy as jnp

D = 8192
FF = 26624
TOKENS = 64


def block_scale(own_key, dims, cuts, low, top_value):
    level = 1.0
    for axis_at, parts in cuts:
        steps = jax.random.uniform(jax.random.fold_in(jax.random.fold_in(own_key, 6), axis_at), (parts,), jnp.float32, low / len(cuts), top_value / len(cuts))
        level = level * jnp.repeat(jnp.exp(steps), dims[axis_at] // parts).reshape((-1,) + (1,) * (len(dims) - 1 - axis_at))
    return level


def scatter_about(key, shape, scale, limit, pieces=(), held_as=jnp.bfloat16):
    gain = block_scale(key, shape, pieces, -0.22, 0.18) if pieces else 1.0
    drawn = jax.random.normal(key, shape, jnp.float32) * scale * gain
    return jnp.minimum(jnp.maximum(drawn, -limit), limit).astype(held_as)


def setup_inputs(seed: int = 0) -> dict:
    arg_keys = jax.random.split(jax.random.key(seed), 7)
    tokens = scatter_about(arg_keys[0], (TOKENS, D), 1.0, 6.0, ((0, 4), (1, 8)))
    gate_weight = scatter_about(arg_keys[1], (D, FF), D ** -0.5, 0.0625, ((0, 8), (1, 4)))
    up_weight = scatter_about(arg_keys[2], (D, FF), D ** -0.5, 0.0625, ((0, 8), (1, 4)))
    down_weight = scatter_about(arg_keys[3], (FF, D), FF ** -0.5, 0.0390625, ((0, 4), (1, 8)))
    gate_tangent = scatter_about(arg_keys[4], (D, FF), D ** -0.5, 0.0625, ((0, 8), (1, 4)))
    up_tangent = scatter_about(arg_keys[5], (D, FF), D ** -0.5, 0.0625, ((0, 8), (1, 4)))
    return {"tokens": tokens, "gate_weight": gate_weight, "up_weight": up_weight, "down_weight": down_weight, "gate_tangent": gate_tangent, "up_tangent": up_tangent}


def matmul(left, right):
    return jnp.dot(left, right, preferred_element_type=jnp.float32)


def silu_terms(gate_sum):
    sigmoid_val = jax.nn.sigmoid(gate_sum)
    return gate_sum * sigmoid_val, sigmoid_val * (1.0 + gate_sum * (1.0 - sigmoid_val))


def reference(tokens, gate_weight, up_weight, down_weight, gate_tangent, up_tangent):
    gate_sum = matmul(tokens, gate_weight)
    up_sum = matmul(tokens, up_weight)
    gate_dir = matmul(tokens, gate_tangent)
    up_dir = matmul(tokens, up_tangent)
    activated, slopes = silu_terms(gate_sum)
    hidden_dir = (slopes * gate_dir * up_sum + activated * up_dir).astype(jnp.bfloat16)
    out_scale = float(TOKENS) ** -0.5
    output_dir = (matmul(hidden_dir, down_weight) * out_scale).astype(jnp.bfloat16)
    back_sum = matmul(output_dir, down_weight.T)
    gate_cot = (back_sum * up_sum * slopes).astype(jnp.bfloat16)
    up_cot = (back_sum * activated).astype(jnp.bfloat16)
    gate_product = matmul(tokens.T, gate_cot).astype(jnp.bfloat16)
    up_product = matmul(tokens.T, up_cot).astype(jnp.bfloat16)
    return gate_product, up_product
```

```python
import functools

import jax
import jax.numpy as jnp
from jax import lax
from jax.experimental import pallas as pl
from jax.experimental.pallas import tpu as pltpu
from jax.sharding import PartitionSpec as P

BF = jnp.bfloat16
F32 = jnp.float32
MESH = pl.DeviceIdType.MESH
SLOTS = 3
CHUNKS = 13
LAG = 1


def curvature_kernel(n, nr, k, names, *refs):
    r = dict(zip(names, refs))
    tokens, weights, down = r["tokens"], [r["gw"], r["uw"], r["gt"], r["ut"]], r["dw"]
    x, w, dn = r["x"], r["w"], r["dn"]
    total, depth = x.shape
    chunk = w.shape[-1]
    half = chunk // 2
    tpo = total // n
    rpr = total // nr
    scale = float(total) ** (-0.5)
    row, me = lax.axis_index("row"), lax.axis_index("col")

    def stride(l, c):
        a = 1 << l
        b = 1 if l == 0 else 1 << (k - l)
        return a if a == b else a + (b - a) * lax.rem(c, 2)

    def bit(l, c):
        return lax.rem(lax.div(me, stride(l, c)), 2)

    def partner(l, c):
        return me + (1 - 2 * bit(l, c)) * stride(l, c)

    def place(c):
        total_place = 0
        for l in range(k):
            total_place = total_place + bit(l, c) * (1 << (k - 1 - l))
        return total_place

    def weight_copy(c, j):
        slot = lax.rem(c, SLOTS)
        cols = pl.ds(pl.multiple_of(c * chunk, chunk), chunk)
        return pltpu.make_async_copy(weights[j].at[:, cols], w.at[slot, j], r["wsem"].at[slot, j])

    def down_copy(c):
        rows = pl.ds(pl.multiple_of(c * chunk, chunk), chunk)
        return pltpu.make_async_copy(down.at[rows], dn.at[c], r["dsem"].at[c])

    def rs_copy(tag, l, c):
        return pltpu.make_async_remote_copy(
            src_ref=r[tag + "s%d" % l].at[c],
            dst_ref=r[tag + "r%d" % l].at[c],
            send_sem=r[tag + "ss"].at[l, c],
            recv_sem=r[tag + "rs"].at[l, c],
            device_id=(row, partner(l, c)),
            device_id_type=MESH,
        )

    def ag_copy(buf, tag, l, c, arriving=False):
        size = 1 << (k - 1 - l)
        base = lax.div(place(c), size) * size
        if arriving:
            base = base + (1 - 2 * bit(l, c)) * size
        part = r[buf].at[c, pl.ds(base, size)]
        return pltpu.make_async_remote_copy(
            src_ref=part,
            dst_ref=part,
            send_sem=r[tag + "sa"].at[l, c],
            recv_sem=r[tag + "ra"].at[l, c],
            device_id=(row, partner(l, c)),
            device_id_type=MESH,
        )

    def ag_wait(buf, tag, l, c):
        ag_copy(buf, tag, l, c).wait_send()
        ag_copy(buf, tag, l, c, arriving=True).wait_recv()

    def rs_step(tag, l, c):
        rs_copy(tag, l, c).wait()
        kept, got = r[tag + "k%d" % l], r[tag + "r%d" % l]
        m = kept.shape[1] // 2
        b = bit(l + 1, c)
        other, mine = pl.ds((1 - b) * m, m), pl.ds(b * m, m)
        r[tag + "s%d" % (l + 1)][c] = (kept[c, other] + got[c, other].astype(F32)).astype(BF)
        rs_copy(tag, l + 1, c).start()
        r[tag + "k%d" % (l + 1)][c] = kept[c, mine] + got[c, mine].astype(F32)

    def rs_last(tag, c):
        rs_copy(tag, k - 1, c).wait()
        return r[tag + "k%d" % (k - 1)][c, 0] + r[tag + "r%d" % (k - 1)][c, 0].astype(F32)

    def peer(d):
        return lax.rem(row + d, nr)

    def source(d):
        return lax.rem(row + nr - d, nr)

    def rows_of(q):
        return pl.ds(pl.multiple_of(q * rpr, rpr), rpr)

    def row_copy(src, dst, tag, d):
        return pltpu.make_async_remote_copy(
            src_ref=src,
            dst_ref=dst,
            send_sem=r[tag + "s"].at[d],
            recv_sem=r[tag + "r"].at[d],
            device_id=(peer(d), me),
            device_id_type=MESH,
        )

    def token_send(d):
        return row_copy(tokens, x.at[rows_of(row)], "t", d)

    def token_arrival(d):
        return row_copy(tokens, x.at[rows_of(source(d))], "t", d)

    own_tokens = pltpu.make_async_copy(tokens, x.at[rows_of(row)], r["osem"])
    own_tokens.start()
    for c in range(SLOTS):
        for j in range(4):
            weight_copy(c, j).start()

    barrier = pltpu.get_barrier_semaphore()
    for l in range(k):
        pl.semaphore_signal(barrier, inc=1, device_id=(row, partner(l, 0)), device_id_type=MESH)
    for d in range(1, nr):
        pl.semaphore_signal(barrier, inc=1, device_id=(peer(d), me), device_id_type=MESH)
    pl.semaphore_wait(barrier, k + nr - 1)

    for d in range(1, nr):
        token_send(d).start()
    own_tokens.wait()
    for d in range(1, nr):
        token_send(d).wait_send()
        token_arrival(d).wait_recv()
    r["acc"][...] = jnp.zeros_like(r["acc"])

    def project(c):
        slot = lax.rem(c, SLOTS)
        pf = r["pf"]
        for j in range(4):
            weight_copy(c, j).wait()
            pf[j] = jnp.dot(x[...], w[slot, j], preferred_element_type=F32)

        @pl.when(c + SLOTS < CHUNKS)
        def _():
            for j in range(4):
                weight_copy(c + SLOTS, j).start()

        down_copy(c).start()
        b = bit(0, c)
        span = total // 2
        for p in range(n // 2):
            rows = pl.ds(pl.multiple_of((1 - b) * span + p * tpo, tpo), tpo)
            r["hs0"][c, p] = jnp.concatenate([pf[j, rows] for j in range(4)], axis=0).astype(BF)
        rs_copy("h", 0, c).start()
        for p in range(n // 2):
            rows = pl.ds(pl.multiple_of(b * span + p * tpo, tpo), tpo)
            r["hk0"][c, p] = jnp.concatenate([pf[j, rows] for j in range(4)], axis=0)

    def hidden(c):
        sums = rs_last("h", c)
        gate_sum, up_sum, gate_dir, up_dir = (sums[j * tpo:(j + 1) * tpo] for j in range(4))
        sig = jax.nn.sigmoid(gate_sum)
        activated = gate_sum * sig
        slopes = sig * (1.0 + gate_sum * (1.0 - sig))
        slope_up = slopes * up_sum
        r["cg"][c] = slope_up
        r["cu"][c] = activated
        hid = slope_up * gate_dir + activated * up_dir
        r["h"][c, place(c)] = jnp.concatenate([hid[:, :half], hid[:, half:]], axis=0).astype(BF)
        ag_copy("h", "h", k - 1, c).start()

    def ag_step(buf, tag, l, c):
        ag_wait(buf, tag, l, c)
        ag_copy(buf, tag, l - 1, c).start()

    def down_part(c):
        ag_wait("h", "h", 0, c)
        down_copy(c).wait()
        got = r["h"][c].astype(F32)
        rows = [jnp.concatenate([got[p, :tpo], got[p, tpo:]], axis=1) for p in range(n)]
        hid = jnp.concatenate(rows, axis=0).astype(BF)
        r["acc"][...] += jnp.dot(hid, dn[c], preferred_element_type=F32)

    def run(stages):
        def step(i, carry):
            for s, stage in enumerate(stages):
                c = i - s * LAG

                @pl.when(jnp.logical_and(c >= 0, c < CHUNKS))
                def _():
                    stage(c)
            return carry

        lax.fori_loop(0, CHUNKS + LAG * (len(stages) - 1), step, 0)

    run(
        [project]
        + [functools.partial(rs_step, "h", l) for l in range(k - 1)]
        + [hidden]
        + [functools.partial(ag_step, "h", "h", l) for l in range(k - 1, 0, -1)]
        + [down_part]
    )

    acc, q, qs, o = r["acc"], r["q"], r["qs"], r["o"]

    def part_send(d):
        return row_copy(qs.at[d], q.at[d], "p", d)

    def out_send(d):
        return row_copy(o.at[rows_of(row)], o.at[rows_of(row)], "o", d)

    def out_arrival(d):
        return row_copy(o.at[rows_of(source(d))], o.at[rows_of(source(d))], "o", d)

    for d in range(1, nr):
        qs[d] = acc[rows_of(peer(d))].astype(BF)
        part_send(d).start()
    out = acc[rows_of(row)]
    for d in range(1, nr):
        part_send(d).wait()
        out = out + q[d].astype(F32)
    o[rows_of(row)] = (out * scale).astype(BF)
    for d in range(1, nr):
        out_send(d).start()
    r["tt"][...] = jnp.transpose(x[...].astype(F32)).astype(BF)
    for d in range(1, nr):
        out_send(d).wait_send()
        out_arrival(d).wait_recv()

    def back(c):
        pb = r["pb"]
        pb[...] = lax.dot_general(
            o[...], dn[c], (((1,), (1,)), ((), ())), preferred_element_type=F32
        )
        b = bit(0, c)
        span = total // 2
        for p in range(n // 2):
            rows = pl.ds(pl.multiple_of((1 - b) * span + p * tpo, tpo), tpo)
            r["bs0"][c, p] = jnp.concatenate([pb[rows, :half], pb[rows, half:]], axis=0).astype(BF)
        rs_copy("b", 0, c).start()
        for p in range(n // 2):
            rows = pl.ds(pl.multiple_of(b * span + p * tpo, tpo), tpo)
            r["bk0"][c, p] = jnp.concatenate([pb[rows, :half], pb[rows, half:]], axis=0)

    def cots(c):
        sums = rs_last("b", c)
        back_sum = jnp.concatenate([sums[:tpo], sums[tpo:]], axis=1)
        both = [back_sum * r["cg"][c], back_sum * r["cu"][c]]
        r["g"][c, place(c)] = jnp.concatenate(both, axis=0).astype(BF)
        ag_copy("g", "b", k - 1, c).start()

    def spread(c):
        ag_wait("g", "b", 0, c)
        got = r["g"][c].astype(F32)
        r["gc"][c] = jnp.concatenate([got[p, :tpo] for p in range(n)], axis=0).astype(BF)
        r["uc"][c] = jnp.concatenate([got[p, tpo:] for p in range(n)], axis=0).astype(BF)

    run(
        [back]
        + [functools.partial(rs_step, "b", l) for l in range(k - 1)]
        + [cots]
        + [functools.partial(ag_step, "g", "b", l) for l in range(k - 1, 0, -1)]
        + [spread]
    )


def product_kernel(tt_ref, gc_ref, uc_ref, gate_ref, up_ref):
    tt = tt_ref[...]
    gate_ref[...] = jnp.dot(tt, gc_ref[0], preferred_element_type=F32).astype(BF)
    up_ref[...] = jnp.dot(tt, uc_ref[0], preferred_element_type=F32).astype(BF)


def body(n, nr, tokens, gate_weight, up_weight, down_weight, gate_tangent, up_tangent):
    k = n.bit_length() - 1
    depth, units = gate_weight.shape
    total = tokens.shape[0] * nr
    chunk = units // CHUNKS
    half = chunk // 2
    tpo = total // n
    dma = pltpu.SemaphoreType.DMA
    vm = pltpu.VMEM
    scratch = [
        ("x", vm((total, depth), BF)),
        ("w", vm((SLOTS, 4, depth, chunk), BF)),
        ("dn", vm((CHUNKS, chunk, depth), BF)),
        ("pf", vm((4, total, chunk), F32)),
        ("pb", vm((total, chunk), F32)),
        ("h", vm((CHUNKS, n, 2 * tpo, half), BF)),
        ("g", vm((CHUNKS, n, 2 * tpo, chunk), BF)),
        ("cg", vm((CHUNKS, tpo, chunk), F32)),
        ("cu", vm((CHUNKS, tpo, chunk), F32)),
        ("acc", vm((total, depth), F32)),
        ("q", vm((nr, total // nr, depth), BF)),
        ("qs", vm((nr, total // nr, depth), BF)),
        ("o", vm((total, depth), BF)),
        ("wsem", dma((SLOTS, 4))),
        ("dsem", dma((CHUNKS,))),
        ("osem", dma),
    ]
    for tag, rows, cols in (("h", 4 * tpo, chunk), ("b", 2 * tpo, half)):
        for l in range(k):
            shape = (CHUNKS, n >> (l + 1), rows, cols)
            scratch += [
                (tag + "k%d" % l, vm(shape, F32)),
                (tag + "s%d" % l, vm(shape, BF)),
                (tag + "r%d" % l, vm(shape, BF)),
            ]
        scratch += [(tag + e, dma((k, CHUNKS))) for e in ("ss", "rs", "sa", "ra")]
    for tag in "tpo":
        scratch += [(tag + e, dma((nr,))) for e in "sr"]
    names = ["tokens", "gw", "uw", "gt", "ut", "dw", "gc", "uc", "tt"] + [s[0] for s in scratch]
    cot = jax.ShapeDtypeStruct((CHUNKS, total, chunk), BF)
    gate_cot, up_cot, tokens_t = pl.pallas_call(
        functools.partial(curvature_kernel, n, nr, k, names),
        out_shape=(cot, cot, jax.ShapeDtypeStruct((depth, total), BF)),
        in_specs=[pl.BlockSpec(memory_space=pl.ANY)] * 6,
        out_specs=[pl.BlockSpec(memory_space=pltpu.VMEM)] * 3,
        scratch_shapes=[s[1] for s in scratch],
        compiler_params=pltpu.CompilerParams(
            collective_id=0, has_side_effects=True, vmem_limit_bytes=60 * 1024 * 1024
        ),
        name="curvature",
    )(tokens, gate_weight, up_weight, gate_tangent, up_tangent, down_weight)
    product = jax.ShapeDtypeStruct((depth, units), BF)
    return pl.pallas_call(
        product_kernel,
        grid=(CHUNKS,),
        out_shape=(product, product),
        in_specs=[
            pl.BlockSpec((depth, total), lambda c: (0, 0)),
            pl.BlockSpec((1, total, chunk), lambda c: (c, 0, 0)),
            pl.BlockSpec((1, total, chunk), lambda c: (c, 0, 0)),
        ],
        out_specs=[pl.BlockSpec((depth, chunk), lambda c: (0, c))] * 2,
        compiler_params=pltpu.CompilerParams(vmem_limit_bytes=32 * 1024 * 1024),
        name="products",
    )(tokens_t, gate_cot, up_cot)


def solution(mesh):
    placed = (
        P("row", "col"),
        P("col", "row"),
        P("col", "row"),
        P("row", "col"),
        P("col", "row"),
        P("col", "row"),
    )
    return jax.shard_map(
        functools.partial(body, mesh.shape["col"], mesh.shape["row"]),
        mesh=mesh,
        in_specs=placed,
        out_specs=(P("col", "row"), P("col", "row")),
        check_vma=False,
    )
```

```python
import functools

import jax
import jax.numpy as jnp
from jax import lax
from jax.experimental import pallas as pl
from jax.experimental.pallas import tpu as pltpu
from jax.sharding import PartitionSpec as P

BF = jnp.bfloat16
F32 = jnp.float32
MESH = pl.DeviceIdType.MESH
SLOTS = 4
CHUNKS = 13
HIDDEN_LAG = 2
BACK_LAG = 3


def curvature_kernel(n, nr, k, names, *refs):
    r = dict(zip(names, refs))
    tokens, weights, down = r["tokens"], [r["gw"], r["uw"], r["gt"], r["ut"]], r["dw"]
    x, w, dn = r["x"], r["w"], r["dn"]
    total, depth = x.shape
    chunk = w.shape[-1]
    half = chunk // 2
    tpo = total // n
    rpr = total // nr
    scale = float(total) ** (-0.5)
    row, me = lax.axis_index("row"), lax.axis_index("col")

    def stride(l, c):
        a = 1 << l
        b = 1 if l == 0 else 1 << (k - l)
        return a if a == b else a + (b - a) * lax.rem(c, 2)

    def bit(l, c):
        return lax.rem(lax.div(me, stride(l, c)), 2)

    def partner(l, c):
        return me + (1 - 2 * bit(l, c)) * stride(l, c)

    def place(c):
        total_place = 0
        for l in range(k):
            total_place = total_place + bit(l, c) * (1 << (k - 1 - l))
        return total_place

    def weight_copy(c, j):
        slot = lax.rem(c, SLOTS)
        cols = pl.ds(pl.multiple_of(c * chunk, chunk), chunk)
        return pltpu.make_async_copy(weights[j].at[:, cols], w.at[slot, j], r["wsem"].at[slot, j])

    def down_copy(c):
        rows = pl.ds(pl.multiple_of(c * chunk, chunk), chunk)
        return pltpu.make_async_copy(down.at[rows], dn.at[c], r["dsem"].at[c])

    def rs_copy(tag, l, c):
        return pltpu.make_async_remote_copy(
            src_ref=r[tag + "s%d" % l].at[c],
            dst_ref=r[tag + "r%d" % l].at[c],
            send_sem=r[tag + "ss"].at[l, c],
            recv_sem=r[tag + "rs"].at[l, c],
            device_id=(row, partner(l, c)),
            device_id_type=MESH,
        )

    def ag_copy(buf, tag, l, c, arriving=False):
        size = 1 << (k - 1 - l)
        base = lax.div(place(c), size) * size
        if arriving:
            base = base + (1 - 2 * bit(l, c)) * size
        part = r[buf].at[c, pl.ds(base, size)]
        return pltpu.make_async_remote_copy(
            src_ref=part,
            dst_ref=part,
            send_sem=r[tag + "sa"].at[l, c],
            recv_sem=r[tag + "ra"].at[l, c],
            device_id=(row, partner(l, c)),
            device_id_type=MESH,
        )

    def ag_wait(buf, tag, l, c):
        ag_copy(buf, tag, l, c).wait_send()
        ag_copy(buf, tag, l, c, arriving=True).wait_recv()

    def rs_step(tag, l, c):
        rs_copy(tag, l, c).wait()
        kept, got = r[tag + "k%d" % l], r[tag + "r%d" % l]
        m = kept.shape[1] // 2
        b = bit(l + 1, c)
        other, mine = pl.ds((1 - b) * m, m), pl.ds(b * m, m)
        r[tag + "s%d" % (l + 1)][c] = (kept[c, other] + got[c, other].astype(F32)).astype(BF)
        rs_copy(tag, l + 1, c).start()
        r[tag + "k%d" % (l + 1)][c] = kept[c, mine] + got[c, mine].astype(F32)

    def rs_last(tag, c):
        rs_copy(tag, k - 1, c).wait()
        return r[tag + "k%d" % (k - 1)][c, 0] + r[tag + "r%d" % (k - 1)][c, 0].astype(F32)

    def peer(d):
        return lax.rem(row + d, nr)

    def source(d):
        return lax.rem(row + nr - d, nr)

    def rows_of(q):
        return pl.ds(pl.multiple_of(q * rpr, rpr), rpr)

    def row_copy(src, dst, tag, d):
        return pltpu.make_async_remote_copy(
            src_ref=src,
            dst_ref=dst,
            send_sem=r[tag + "s"].at[d],
            recv_sem=r[tag + "r"].at[d],
            device_id=(peer(d), me),
            device_id_type=MESH,
        )

    def token_send(d):
        return row_copy(tokens, x.at[rows_of(row)], "t", d)

    def token_arrival(d):
        return row_copy(tokens, x.at[rows_of(source(d))], "t", d)

    own_tokens = pltpu.make_async_copy(tokens, x.at[rows_of(row)], r["osem"])
    own_tokens.start()
    for c in range(SLOTS):
        for j in range(4):
            weight_copy(c, j).start()

    barrier = pltpu.get_barrier_semaphore()
    for l in range(k):
        pl.semaphore_signal(barrier, inc=1, device_id=(row, partner(l, 0)), device_id_type=MESH)
    for d in range(1, nr):
        pl.semaphore_signal(barrier, inc=1, device_id=(peer(d), me), device_id_type=MESH)
    pl.semaphore_wait(barrier, k + nr - 1)

    for d in range(1, nr):
        token_send(d).start()
    own_tokens.wait()
    for d in range(1, nr):
        token_send(d).wait_send()
        token_arrival(d).wait_recv()
    r["acc"][...] = jnp.zeros_like(r["acc"])

    def project(c):
        slot = lax.rem(c, SLOTS)
        pf = r["pf"]
        for j in range(4):
            weight_copy(c, j).wait()
            pf[j] = jnp.dot(x[...], w[slot, j], preferred_element_type=F32)

        @pl.when(c + SLOTS < CHUNKS)
        def _():
            for j in range(4):
                weight_copy(c + SLOTS, j).start()

        down_copy(c).start()
        b = bit(0, c)
        span = total // 2
        for p in range(n // 2):
            rows = pl.ds(pl.multiple_of((1 - b) * span + p * tpo, tpo), tpo)
            r["hs0"][c, p] = jnp.concatenate([pf[j, rows] for j in range(4)], axis=0).astype(BF)
        rs_copy("h", 0, c).start()
        for p in range(n // 2):
            rows = pl.ds(pl.multiple_of(b * span + p * tpo, tpo), tpo)
            r["hk0"][c, p] = jnp.concatenate([pf[j, rows] for j in range(4)], axis=0)

    def hidden(c):
        sums = rs_last("h", c)
        gate_sum, up_sum, gate_dir, up_dir = (sums[j * tpo:(j + 1) * tpo] for j in range(4))
        sig = jax.nn.sigmoid(gate_sum)
        activated = gate_sum * sig
        slopes = sig * (1.0 + gate_sum * (1.0 - sig))
        slope_up = slopes * up_sum
        r["cg"][c] = slope_up
        r["cu"][c] = activated
        hid = slope_up * gate_dir + activated * up_dir
        r["h"][c, place(c)] = jnp.concatenate([hid[:, :half], hid[:, half:]], axis=0).astype(BF)
        ag_copy("h", "h", k - 1, c).start()

    def ag_step(buf, tag, l, c):
        ag_wait(buf, tag, l, c)
        ag_copy(buf, tag, l - 1, c).start()

    def down_part(c):
        ag_wait("h", "h", 0, c)
        down_copy(c).wait()
        got = r["h"][c].astype(F32)
        rows = [jnp.concatenate([got[p, :tpo], got[p, tpo:]], axis=1) for p in range(n)]
        hid = jnp.concatenate(rows, axis=0).astype(BF)
        r["acc"][...] += jnp.dot(hid, dn[c], preferred_element_type=F32)

    def run(lag, stages):
        def step(i, carry):
            for s, stage in enumerate(stages):
                c = i - s * lag

                @pl.when(jnp.logical_and(c >= 0, c < CHUNKS))
                def _():
                    stage(c)
            return carry

        lax.fori_loop(0, CHUNKS + lag * (len(stages) - 1), step, 0)

    run(
        HIDDEN_LAG,
        [project]
        + [functools.partial(rs_step, "h", l) for l in range(k - 1)]
        + [hidden]
        + [functools.partial(ag_step, "h", "h", l) for l in range(k - 1, 0, -1)]
        + [down_part],
    )

    acc, q, qs, o = r["acc"], r["q"], r["qs"], r["o"]

    def part_send(d):
        return row_copy(qs.at[d], q.at[d], "p", d)

    def out_send(d):
        return row_copy(o.at[rows_of(row)], o.at[rows_of(row)], "o", d)

    def out_arrival(d):
        return row_copy(o.at[rows_of(source(d))], o.at[rows_of(source(d))], "o", d)

    for d in range(1, nr):
        qs[d] = acc[rows_of(peer(d))].astype(BF)
        part_send(d).start()
    out = acc[rows_of(row)]
    for d in range(1, nr):
        part_send(d).wait()
        out = out + q[d].astype(F32)
    o[rows_of(row)] = (out * scale).astype(BF)
    for d in range(1, nr):
        out_send(d).start()
    r["tt"][...] = jnp.transpose(x[...].astype(F32)).astype(BF)
    for d in range(1, nr):
        out_send(d).wait_send()
        out_arrival(d).wait_recv()

    def back(c):
        pb = r["pb"]
        pb[...] = lax.dot_general(
            o[...], dn[c], (((1,), (1,)), ((), ())), preferred_element_type=F32
        )
        b = bit(0, c)
        span = total // 2
        for p in range(n // 2):
            rows = pl.ds(pl.multiple_of((1 - b) * span + p * tpo, tpo), tpo)
            r["bs0"][c, p] = jnp.concatenate([pb[rows, :half], pb[rows, half:]], axis=0).astype(BF)
        rs_copy("b", 0, c).start()
        for p in range(n // 2):
            rows = pl.ds(pl.multiple_of(b * span + p * tpo, tpo), tpo)
            r["bk0"][c, p] = jnp.concatenate([pb[rows, :half], pb[rows, half:]], axis=0)

    def cots(c):
        sums = rs_last("b", c)
        back_sum = jnp.concatenate([sums[:tpo], sums[tpo:]], axis=1)
        both = [back_sum * r["cg"][c], back_sum * r["cu"][c]]
        r["g"][c, place(c)] = jnp.concatenate(both, axis=0).astype(BF)
        ag_copy("g", "b", k - 1, c).start()

    def spread(c):
        ag_wait("g", "b", 0, c)
        got = r["g"][c].astype(F32)
        r["gc"][c] = jnp.concatenate([got[p, :tpo] for p in range(n)], axis=0).astype(BF)
        r["uc"][c] = jnp.concatenate([got[p, tpo:] for p in range(n)], axis=0).astype(BF)

    run(
        BACK_LAG,
        [back]
        + [functools.partial(rs_step, "b", l) for l in range(k - 1)]
        + [cots]
        + [functools.partial(ag_step, "g", "b", l) for l in range(k - 1, 0, -1)]
        + [spread],
    )


def product_kernel(tt_ref, gc_ref, uc_ref, gate_ref, up_ref):
    tt = tt_ref[...]
    gate_ref[...] = jnp.dot(tt, gc_ref[0], preferred_element_type=F32).astype(BF)
    up_ref[...] = jnp.dot(tt, uc_ref[0], preferred_element_type=F32).astype(BF)


def body(n, nr, tokens, gate_weight, up_weight, down_weight, gate_tangent, up_tangent):
    k = n.bit_length() - 1
    depth, units = gate_weight.shape
    total = tokens.shape[0] * nr
    chunk = units // CHUNKS
    half = chunk // 2
    tpo = total // n
    dma = pltpu.SemaphoreType.DMA
    vm = pltpu.VMEM
    scratch = [
        ("x", vm((total, depth), BF)),
        ("w", vm((SLOTS, 4, depth, chunk), BF)),
        ("dn", vm((CHUNKS, chunk, depth), BF)),
        ("pf", vm((4, total, chunk), F32)),
        ("pb", vm((total, chunk), F32)),
        ("h", vm((CHUNKS, n, 2 * tpo, half), BF)),
        ("g", vm((CHUNKS, n, 2 * tpo, chunk), BF)),
        ("cg", vm((CHUNKS, tpo, chunk), F32)),
        ("cu", vm((CHUNKS, tpo, chunk), F32)),
        ("acc", vm((total, depth), F32)),
        ("q", vm((nr, total // nr, depth), BF)),
        ("qs", vm((nr, total // nr, depth), BF)),
        ("o", vm((total, depth), BF)),
        ("wsem", dma((SLOTS, 4))),
        ("dsem", dma((CHUNKS,))),
        ("osem", dma),
    ]
    for tag, rows, cols in (("h", 4 * tpo, chunk), ("b", 2 * tpo, half)):
        for l in range(k):
            shape = (CHUNKS, n >> (l + 1), rows, cols)
            scratch += [
                (tag + "k%d" % l, vm(shape, F32)),
                (tag + "s%d" % l, vm(shape, BF)),
                (tag + "r%d" % l, vm(shape, BF)),
            ]
        scratch += [(tag + e, dma((k, CHUNKS))) for e in ("ss", "rs", "sa", "ra")]
    for tag in "tpo":
        scratch += [(tag + e, dma((nr,))) for e in "sr"]
    names = ["tokens", "gw", "uw", "gt", "ut", "dw", "gc", "uc", "tt"] + [s[0] for s in scratch]
    cot = jax.ShapeDtypeStruct((CHUNKS, total, chunk), BF)
    gate_cot, up_cot, tokens_t = pl.pallas_call(
        functools.partial(curvature_kernel, n, nr, k, names),
        out_shape=(cot, cot, jax.ShapeDtypeStruct((depth, total), BF)),
        in_specs=[pl.BlockSpec(memory_space=pl.ANY)] * 6,
        out_specs=[pl.BlockSpec(memory_space=pltpu.VMEM)] * 3,
        scratch_shapes=[s[1] for s in scratch],
        compiler_params=pltpu.CompilerParams(
            collective_id=0, has_side_effects=True, vmem_limit_bytes=60 * 1024 * 1024
        ),
        name="curvature",
    )(tokens, gate_weight, up_weight, gate_tangent, up_tangent, down_weight)
    product = jax.ShapeDtypeStruct((depth, units), BF)
    return pl.pallas_call(
        product_kernel,
        grid=(CHUNKS,),
        out_shape=(product, product),
        in_specs=[
            pl.BlockSpec((depth, total), lambda c: (0, 0)),
            pl.BlockSpec((1, total, chunk), lambda c: (c, 0, 0)),
            pl.BlockSpec((1, total, chunk), lambda c: (c, 0, 0)),
        ],
        out_specs=[pl.BlockSpec((depth, chunk), lambda c: (0, c))] * 2,
        compiler_params=pltpu.CompilerParams(vmem_limit_bytes=60 * 1024 * 1024),
        name="products",
    )(tokens_t, gate_cot, up_cot)


def solution(mesh):
    placed = (
        P("row", "col"),
        P("col", "row"),
        P("col", "row"),
        P("row", "col"),
        P("col", "row"),
        P("col", "row"),
    )
    return jax.shard_map(
        functools.partial(body, mesh.shape["col"], mesh.shape["row"]),
        mesh=mesh,
        in_specs=placed,
        out_specs=(P("col", "row"), P("col", "row")),
        check_vma=False,
    )
```

```python
import functools

import jax
import jax.numpy as jnp
from jax import lax
from jax.experimental import pallas as pl
from jax.experimental.pallas import tpu as pltpu
from jax.sharding import PartitionSpec as P

BF = jnp.bfloat16
F32 = jnp.float32
MESH = pl.DeviceIdType.MESH
SLOTS = 4
CHUNKS = 13
HIDDEN_LAG = 2
BACK_LAG = 2
GROUPS = ((0, 2, 4, 6), (1, 3, 5), (8, 10, 12), (7, 9, 11))


def curvature_kernel(n, nr, k, names, *refs):
    r = dict(zip(names, refs))
    tokens, weights, down = r["tokens"], [r["gw"], r["uw"], r["gt"], r["ut"]], r["dw"]
    x, w, dn = r["x"], r["w"], r["dn"]
    total, depth = x.shape
    chunk = w.shape[-1]
    half = chunk // 2
    tpo = total // n
    rpr = total // nr
    scale = float(total) ** (-0.5)
    row, me = lax.axis_index("row"), lax.axis_index("col")

    def stride(l, c):
        a = 1 << l
        b = 1 if l == 0 else 1 << (k - l)
        odd = c % 2 if isinstance(c, int) else lax.rem(c, 2)
        return a if a == b else a + (b - a) * odd

    def bit(l, c):
        return lax.rem(lax.div(me, stride(l, c)), 2)

    def partner(l, c):
        return me + (1 - 2 * bit(l, c)) * stride(l, c)

    def place(c):
        total_place = 0
        for l in range(k):
            total_place = total_place + bit(l, c) * (1 << (k - 1 - l))
        return total_place

    def weight_copy(c, j):
        slot = lax.rem(c, SLOTS)
        cols = pl.ds(pl.multiple_of(c * chunk, chunk), chunk)
        return pltpu.make_async_copy(weights[j].at[:, cols], w.at[slot, j], r["wsem"].at[slot, j])

    def down_copy(c):
        rows = pl.ds(pl.multiple_of(c * chunk, chunk), chunk)
        return pltpu.make_async_copy(down.at[rows], dn.at[c], r["dsem"].at[c])

    def rs_copy(tag, l, c):
        return pltpu.make_async_remote_copy(
            src_ref=r[tag + "s%d" % l].at[c],
            dst_ref=r[tag + "r%d" % l].at[c],
            send_sem=r[tag + "ss"].at[l, c],
            recv_sem=r[tag + "rs"].at[l, c],
            device_id=(row, partner(l, c)),
            device_id_type=MESH,
        )

    def ag_copy(buf, tag, l, c, arriving=False):
        size = 1 << (k - 1 - l)
        base = lax.div(place(c), size) * size
        if arriving:
            base = base + (1 - 2 * bit(l, c)) * size
        part = r[buf].at[c, pl.ds(base, size)]
        return pltpu.make_async_remote_copy(
            src_ref=part,
            dst_ref=part,
            send_sem=r[tag + "sa"].at[l, c],
            recv_sem=r[tag + "ra"].at[l, c],
            device_id=(row, partner(l, c)),
            device_id_type=MESH,
        )

    def ag_wait(buf, tag, l, c):
        ag_copy(buf, tag, l, c).wait_send()
        ag_copy(buf, tag, l, c, arriving=True).wait_recv()

    def rs_step(tag, l, c):
        rs_copy(tag, l, c).wait()
        kept, got = r[tag + "k%d" % l], r[tag + "r%d" % l]
        m = kept.shape[1] // 2
        b = bit(l + 1, c)
        other, mine = pl.ds((1 - b) * m, m), pl.ds(b * m, m)
        r[tag + "s%d" % (l + 1)][c] = (kept[c, other] + got[c, other].astype(F32)).astype(BF)
        rs_copy(tag, l + 1, c).start()
        r[tag + "k%d" % (l + 1)][c] = kept[c, mine] + got[c, mine].astype(F32)

    def rs_last(tag, c):
        rs_copy(tag, k - 1, c).wait()
        return r[tag + "k%d" % (k - 1)][c, 0] + r[tag + "r%d" % (k - 1)][c, 0].astype(F32)

    def peer(d):
        return lax.rem(row + d, nr)

    def source(d):
        return lax.rem(row + nr - d, nr)

    def rows_of(q):
        return pl.ds(pl.multiple_of(q * rpr, rpr), rpr)

    def row_copy(src, dst, tag, d):
        return pltpu.make_async_remote_copy(
            src_ref=src,
            dst_ref=dst,
            send_sem=r[tag + "s"].at[d],
            recv_sem=r[tag + "r"].at[d],
            device_id=(peer(d), me),
            device_id_type=MESH,
        )

    def token_send(d):
        return row_copy(tokens, x.at[rows_of(row)], "t", d)

    def token_arrival(d):
        return row_copy(tokens, x.at[rows_of(source(d))], "t", d)

    own_tokens = pltpu.make_async_copy(tokens, x.at[rows_of(row)], r["osem"])
    own_tokens.start()
    for c in range(SLOTS):
        for j in range(4):
            weight_copy(c, j).start()

    barrier = pltpu.get_barrier_semaphore()
    for l in range(k):
        pl.semaphore_signal(barrier, inc=1, device_id=(row, partner(l, 0)), device_id_type=MESH)
    for d in range(1, nr):
        pl.semaphore_signal(barrier, inc=1, device_id=(peer(d), me), device_id_type=MESH)
    pl.semaphore_wait(barrier, k + nr - 1)

    for d in range(1, nr):
        token_send(d).start()
    own_tokens.wait()
    for d in range(1, nr):
        token_send(d).wait_send()
        token_arrival(d).wait_recv()
    r["acc"][...] = jnp.zeros_like(r["acc"])

    def project(c):
        slot = lax.rem(c, SLOTS)
        pf = r["pf"]
        for j in range(4):
            weight_copy(c, j).wait()
            pf[j] = jnp.dot(x[...], w[slot, j], preferred_element_type=F32)

        @pl.when(c + SLOTS < CHUNKS)
        def _():
            for j in range(4):
                weight_copy(c + SLOTS, j).start()

        down_copy(c).start()
        b = bit(0, c)
        span = total // 2
        for p in range(n // 2):
            rows = pl.ds(pl.multiple_of((1 - b) * span + p * tpo, tpo), tpo)
            r["hs0"][c, p] = jnp.concatenate([pf[j, rows] for j in range(4)], axis=0).astype(BF)
        rs_copy("h", 0, c).start()
        for p in range(n // 2):
            rows = pl.ds(pl.multiple_of(b * span + p * tpo, tpo), tpo)
            r["hk0"][c, p] = jnp.concatenate([pf[j, rows] for j in range(4)], axis=0)

    def hidden(c):
        sums = rs_last("h", c)
        gate_sum, up_sum, gate_dir, up_dir = (sums[j * tpo:(j + 1) * tpo] for j in range(4))
        sig = jax.nn.sigmoid(gate_sum)
        activated = gate_sum * sig
        slopes = sig * (1.0 + gate_sum * (1.0 - sig))
        slope_up = slopes * up_sum
        r["cg"][c] = slope_up
        r["cu"][c] = activated
        hid = slope_up * gate_dir + activated * up_dir
        r["h"][c, place(c)] = jnp.concatenate([hid[:, :half], hid[:, half:]], axis=0).astype(BF)
        ag_copy("h", "h", k - 1, c).start()

    def ag_step(buf, tag, l, c):
        ag_wait(buf, tag, l, c)
        ag_copy(buf, tag, l - 1, c).start()

    def down_part(c):
        ag_wait("h", "h", 0, c)
        down_copy(c).wait()
        got = r["h"][c].astype(F32)
        rows = [jnp.concatenate([got[p, :tpo], got[p, tpo:]], axis=1) for p in range(n)]
        hid = jnp.concatenate(rows, axis=0).astype(BF)
        r["acc"][...] += jnp.dot(hid, dn[c], preferred_element_type=F32)

    def run(lag, stages):
        def step(i, carry):
            for s, stage in enumerate(stages):
                c = i - s * lag

                @pl.when(jnp.logical_and(c >= 0, c < CHUNKS))
                def _():
                    stage(c)
            return carry

        lax.fori_loop(0, CHUNKS + lag * (len(stages) - 1), step, 0)

    run(
        HIDDEN_LAG,
        [project]
        + [functools.partial(rs_step, "h", l) for l in range(k - 1)]
        + [hidden]
        + [functools.partial(ag_step, "h", "h", l) for l in range(k - 1, 0, -1)]
        + [down_part],
    )

    acc, q, qs, o = r["acc"], r["q"], r["qs"], r["o"]

    def part_send(d):
        return row_copy(qs.at[d], q.at[d], "p", d)

    def out_send(d):
        return row_copy(o.at[rows_of(row)], o.at[rows_of(row)], "o", d)

    def out_arrival(d):
        return row_copy(o.at[rows_of(source(d))], o.at[rows_of(source(d))], "o", d)

    for d in range(1, nr):
        qs[d] = acc[rows_of(peer(d))].astype(BF)
        part_send(d).start()
    out = acc[rows_of(row)]
    for d in range(1, nr):
        part_send(d).wait()
        out = out + q[d].astype(F32)
    o[rows_of(row)] = (out * scale).astype(BF)
    for d in range(1, nr):
        out_send(d).start()
    r["tt"][...] = jnp.transpose(x[...].astype(F32)).astype(BF)
    for d in range(1, nr):
        out_send(d).wait_send()
        out_arrival(d).wait_recv()

    starts = [sum(len(g) for g in GROUPS[:i]) for i in range(len(GROUPS))]

    def held(g):
        return pl.ds(starts[g], len(GROUPS[g]))

    def back_copy(l, g):
        c = GROUPS[g][0]
        return pltpu.make_async_remote_copy(
            src_ref=r["bs%d" % l].at[held(g)],
            dst_ref=r["br%d" % l].at[held(g)],
            send_sem=r["bss"].at[l, g],
            recv_sem=r["brs"].at[l, g],
            device_id=(row, partner(l, c)),
            device_id_type=MESH,
        )

    def cot_copy(l, g, arriving=False):
        c = GROUPS[g][0]
        size = 1 << (k - 1 - l)
        base = lax.div(place(c), size) * size
        if arriving:
            base = base + (1 - 2 * bit(l, c)) * size
        part = r["g"].at[held(g), pl.ds(base, size)]
        return pltpu.make_async_remote_copy(
            src_ref=part,
            dst_ref=part,
            send_sem=r["bsa"].at[l, g],
            recv_sem=r["bra"].at[l, g],
            device_id=(row, partner(l, c)),
            device_id_type=MESH,
        )

    def cot_wait(l, g):
        cot_copy(l, g).wait_send()
        cot_copy(l, g, arriving=True).wait_recv()

    def back(g):
        pb = r["pb"]
        b = bit(0, 0)
        span = total // 2
        for i, c in enumerate(GROUPS[g]):
            at = starts[g] + i
            pb[i] = lax.dot_general(
                o[...], dn[c], (((1,), (1,)), ((), ())), preferred_element_type=F32
            )
            for p in range(n // 2):
                rows = pl.ds(pl.multiple_of((1 - b) * span + p * tpo, tpo), tpo)
                both = [pb[i, rows, :half], pb[i, rows, half:]]
                r["bs0"][at, p] = jnp.concatenate(both, axis=0).astype(BF)
        back_copy(0, g).start()
        for i, c in enumerate(GROUPS[g]):
            at = starts[g] + i
            for p in range(n // 2):
                rows = pl.ds(pl.multiple_of(b * span + p * tpo, tpo), tpo)
                both = [pb[i, rows, :half], pb[i, rows, half:]]
                r["bk0"][at, p] = jnp.concatenate(both, axis=0)

    def back_step(l, g):
        back_copy(l, g).wait()
        kept, got = r["bk%d" % l], r["br%d" % l]
        m = kept.shape[1] // 2
        b = bit(l + 1, GROUPS[g][0])
        other, mine = pl.ds((1 - b) * m, m), pl.ds(b * m, m)
        at = held(g)
        r["bs%d" % (l + 1)][at] = (kept[at, other] + got[at, other].astype(F32)).astype(BF)
        back_copy(l + 1, g).start()
        r["bk%d" % (l + 1)][at] = kept[at, mine] + got[at, mine].astype(F32)

    def cots(g):
        back_copy(k - 1, g).wait()
        for i, c in enumerate(GROUPS[g]):
            at = starts[g] + i
            sums = r["bk%d" % (k - 1)][at, 0] + r["br%d" % (k - 1)][at, 0].astype(F32)
            back_sum = jnp.concatenate([sums[:tpo], sums[tpo:]], axis=1)
            both = [back_sum * r["cg"][c], back_sum * r["cu"][c]]
            r["g"][at, place(c)] = jnp.concatenate(both, axis=0).astype(BF)
        cot_copy(k - 1, g).start()

    def cot_step(l, g):
        cot_wait(l, g)
        cot_copy(l - 1, g).start()

    def spread(g):
        cot_wait(0, g)
        for i, c in enumerate(GROUPS[g]):
            got = r["g"][starts[g] + i].astype(F32)
            r["gc"][c] = jnp.concatenate([got[p, :tpo] for p in range(n)], axis=0).astype(BF)
            r["uc"][c] = jnp.concatenate([got[p, tpo:] for p in range(n)], axis=0).astype(BF)

    stages = [back]
    stages += [functools.partial(back_step, l) for l in range(k - 1)]
    stages += [cots]
    stages += [functools.partial(cot_step, l) for l in range(k - 1, 0, -1)]
    stages += [spread]
    for i in range(len(GROUPS) + BACK_LAG * (len(stages) - 1)):
        for s, stage in enumerate(stages):
            g = i - s * BACK_LAG
            if 0 <= g < len(GROUPS):
                stage(g)


def product_kernel(tt_ref, gc_ref, uc_ref, gate_ref, up_ref):
    tt = tt_ref[...]
    gate_ref[...] = jnp.dot(tt, gc_ref[0], preferred_element_type=F32).astype(BF)
    up_ref[...] = jnp.dot(tt, uc_ref[0], preferred_element_type=F32).astype(BF)


def body(n, nr, tokens, gate_weight, up_weight, down_weight, gate_tangent, up_tangent):
    k = n.bit_length() - 1
    depth, units = gate_weight.shape
    total = tokens.shape[0] * nr
    chunk = units // CHUNKS
    half = chunk // 2
    tpo = total // n
    dma = pltpu.SemaphoreType.DMA
    vm = pltpu.VMEM
    scratch = [
        ("x", vm((total, depth), BF)),
        ("w", vm((SLOTS, 4, depth, chunk), BF)),
        ("dn", vm((CHUNKS, chunk, depth), BF)),
        ("pf", vm((4, total, chunk), F32)),
        ("pb", vm((max(len(g) for g in GROUPS), total, chunk), F32)),
        ("h", vm((CHUNKS, n, 2 * tpo, half), BF)),
        ("g", vm((CHUNKS, n, 2 * tpo, chunk), BF)),
        ("cg", vm((CHUNKS, tpo, chunk), F32)),
        ("cu", vm((CHUNKS, tpo, chunk), F32)),
        ("acc", vm((total, depth), F32)),
        ("q", vm((nr, total // nr, depth), BF)),
        ("qs", vm((nr, total // nr, depth), BF)),
        ("o", vm((total, depth), BF)),
        ("wsem", dma((SLOTS, 4))),
        ("dsem", dma((CHUNKS,))),
        ("osem", dma),
    ]
    for tag, rows, cols in (("h", 4 * tpo, chunk), ("b", 2 * tpo, half)):
        for l in range(k):
            shape = (CHUNKS, n >> (l + 1), rows, cols)
            scratch += [
                (tag + "k%d" % l, vm(shape, F32)),
                (tag + "s%d" % l, vm(shape, BF)),
                (tag + "r%d" % l, vm(shape, BF)),
            ]
        scratch += [(tag + e, dma((k, CHUNKS))) for e in ("ss", "rs", "sa", "ra")]
    for tag in "tpo":
        scratch += [(tag + e, dma((nr,))) for e in "sr"]
    names = ["tokens", "gw", "uw", "gt", "ut", "dw", "gc", "uc", "tt"] + [s[0] for s in scratch]
    cot = jax.ShapeDtypeStruct((CHUNKS, total, chunk), BF)
    gate_cot, up_cot, tokens_t = pl.pallas_call(
        functools.partial(curvature_kernel, n, nr, k, names),
        out_shape=(cot, cot, jax.ShapeDtypeStruct((depth, total), BF)),
        in_specs=[pl.BlockSpec(memory_space=pl.ANY)] * 6,
        out_specs=[pl.BlockSpec(memory_space=pltpu.VMEM)] * 3,
        scratch_shapes=[s[1] for s in scratch],
        compiler_params=pltpu.CompilerParams(
            collective_id=0, has_side_effects=True, vmem_limit_bytes=60 * 1024 * 1024
        ),
        name="curvature",
    )(tokens, gate_weight, up_weight, gate_tangent, up_tangent, down_weight)
    product = jax.ShapeDtypeStruct((depth, units), BF)
    return pl.pallas_call(
        product_kernel,
        grid=(CHUNKS,),
        out_shape=(product, product),
        in_specs=[
            pl.BlockSpec((depth, total), lambda c: (0, 0)),
            pl.BlockSpec((1, total, chunk), lambda c: (c, 0, 0)),
            pl.BlockSpec((1, total, chunk), lambda c: (c, 0, 0)),
        ],
        out_specs=[pl.BlockSpec((depth, chunk), lambda c: (0, c))] * 2,
        compiler_params=pltpu.CompilerParams(vmem_limit_bytes=60 * 1024 * 1024),
        name="products",
    )(tokens_t, gate_cot, up_cot)


def solution(mesh):
    placed = (
        P("row", "col"),
        P("col", "row"),
        P("col", "row"),
        P("row", "col"),
        P("col", "row"),
        P("col", "row"),
    )
    return jax.shard_map(
        functools.partial(body, mesh.shape["col"], mesh.shape["row"]),
        mesh=mesh,
        in_specs=placed,
        out_specs=(P("col", "row"), P("col", "row")),
        check_vma=False,
    )
```

```python
import functools

import jax
import jax.numpy as jnp
from jax import lax
from jax.experimental import pallas as pl
from jax.experimental.pallas import tpu as pltpu
from jax.sharding import PartitionSpec as P

BF = jnp.bfloat16
F32 = jnp.float32
MESH = pl.DeviceIdType.MESH
SLOTS = 4
CHUNKS = 13
BACK_LAG = 2
GROUPS = ((0, 2, 4, 6), (1, 3, 5), (8, 10, 12), (7, 9, 11))


def curvature_kernel(n, nr, k, names, *refs):
    r = dict(zip(names, refs))
    tokens, weights, down = r["tokens"], [r["gw"], r["uw"], r["gt"], r["ut"]], r["dw"]
    x, w, dn = r["x"], r["w"], r["dn"]
    total, depth = x.shape
    chunk = w.shape[-1]
    half = chunk // 2
    tpo = total // n
    rpr = total // nr
    scale = float(total) ** (-0.5)
    row, me = lax.axis_index("row"), lax.axis_index("col")

    def stride(l, c):
        a = 1 << l
        b = 1 if l == 0 else 1 << (k - l)
        odd = c % 2 if isinstance(c, int) else lax.rem(c, 2)
        return a if a == b else a + (b - a) * odd

    def bit(l, c):
        return lax.rem(lax.div(me, stride(l, c)), 2)

    def partner(l, c):
        return me + (1 - 2 * bit(l, c)) * stride(l, c)

    def place(c):
        total_place = 0
        for l in range(k):
            total_place = total_place + bit(l, c) * (1 << (k - 1 - l))
        return total_place

    def weight_copy(c, j):
        slot = lax.rem(c, SLOTS)
        cols = pl.ds(pl.multiple_of(c * chunk, chunk), chunk)
        return pltpu.make_async_copy(weights[j].at[:, cols], w.at[slot, j], r["wsem"].at[slot, j])

    def down_copy(c):
        rows = pl.ds(pl.multiple_of(c * chunk, chunk), chunk)
        return pltpu.make_async_copy(down.at[rows], dn.at[c], r["dsem"].at[c])

    def rs_copy(tag, l, c):
        return pltpu.make_async_remote_copy(
            src_ref=r[tag + "s%d" % l].at[c],
            dst_ref=r[tag + "r%d" % l].at[c],
            send_sem=r[tag + "ss"].at[l, c],
            recv_sem=r[tag + "rs"].at[l, c],
            device_id=(row, partner(l, c)),
            device_id_type=MESH,
        )

    def ag_copy(buf, tag, l, c, arriving=False):
        size = 1 << (k - 1 - l)
        base = lax.div(place(c), size) * size
        if arriving:
            base = base + (1 - 2 * bit(l, c)) * size
        part = r[buf].at[c, pl.ds(base, size)]
        return pltpu.make_async_remote_copy(
            src_ref=part,
            dst_ref=part,
            send_sem=r[tag + "sa"].at[l, c],
            recv_sem=r[tag + "ra"].at[l, c],
            device_id=(row, partner(l, c)),
            device_id_type=MESH,
        )

    def ag_wait(buf, tag, l, c):
        ag_copy(buf, tag, l, c).wait_send()
        ag_copy(buf, tag, l, c, arriving=True).wait_recv()

    def rs_step(tag, l, c):
        rs_copy(tag, l, c).wait()
        kept, got = r[tag + "k%d" % l], r[tag + "r%d" % l]
        m = kept.shape[1] // 2
        b = bit(l + 1, c)
        other, mine = pl.ds((1 - b) * m, m), pl.ds(b * m, m)
        r[tag + "s%d" % (l + 1)][c] = (kept[c, other] + got[c, other].astype(F32)).astype(BF)
        rs_copy(tag, l + 1, c).start()
        r[tag + "k%d" % (l + 1)][c] = kept[c, mine] + got[c, mine].astype(F32)

    def rs_last(tag, c):
        rs_copy(tag, k - 1, c).wait()
        return r[tag + "k%d" % (k - 1)][c, 0] + r[tag + "r%d" % (k - 1)][c, 0].astype(F32)

    def peer(d):
        return lax.rem(row + d, nr)

    def source(d):
        return lax.rem(row + nr - d, nr)

    def rows_of(q):
        return pl.ds(pl.multiple_of(q * rpr, rpr), rpr)

    def row_copy(src, dst, tag, d):
        return pltpu.make_async_remote_copy(
            src_ref=src,
            dst_ref=dst,
            send_sem=r[tag + "s"].at[d],
            recv_sem=r[tag + "r"].at[d],
            device_id=(peer(d), me),
            device_id_type=MESH,
        )

    def token_send(d):
        return row_copy(tokens, x.at[rows_of(row)], "t", d)

    def token_arrival(d):
        return row_copy(tokens, x.at[rows_of(source(d))], "t", d)

    own_tokens = pltpu.make_async_copy(tokens, x.at[rows_of(row)], r["osem"])
    own_tokens.start()
    for c in range(SLOTS):
        for j in range(4):
            weight_copy(c, j).start()

    barrier = pltpu.get_barrier_semaphore()
    for l in range(k):
        pl.semaphore_signal(barrier, inc=1, device_id=(row, partner(l, 0)), device_id_type=MESH)
    for d in range(1, nr):
        pl.semaphore_signal(barrier, inc=1, device_id=(peer(d), me), device_id_type=MESH)
    pl.semaphore_wait(barrier, k + nr - 1)

    for d in range(1, nr):
        token_send(d).start()
    own_tokens.wait()
    for d in range(1, nr):
        token_send(d).wait_send()
        token_arrival(d).wait_recv()
    r["acc"][...] = jnp.zeros_like(r["acc"])

    def project(c):
        slot = lax.rem(c, SLOTS)
        pf = r["pf"]
        for j in range(4):
            weight_copy(c, j).wait()
            pf[j] = jnp.dot(x[...], w[slot, j], preferred_element_type=F32)

        @pl.when(c + SLOTS < CHUNKS)
        def _():
            for j in range(4):
                weight_copy(c + SLOTS, j).start()

        down_copy(c).start()
        b = bit(0, c)
        span = total // 2
        for p in range(n // 2):
            rows = pl.ds(pl.multiple_of((1 - b) * span + p * tpo, tpo), tpo)
            r["hs0"][c, p] = jnp.concatenate([pf[j, rows] for j in range(4)], axis=0).astype(BF)
        rs_copy("h", 0, c).start()
        for p in range(n // 2):
            rows = pl.ds(pl.multiple_of(b * span + p * tpo, tpo), tpo)
            r["hk0"][c, p] = jnp.concatenate([pf[j, rows] for j in range(4)], axis=0)

    def hidden(c):
        sums = rs_last("h", c)
        gate_sum, up_sum, gate_dir, up_dir = (sums[j * tpo:(j + 1) * tpo] for j in range(4))
        sig = jax.nn.sigmoid(gate_sum)
        activated = gate_sum * sig
        slopes = sig * (1.0 + gate_sum * (1.0 - sig))
        slope_up = slopes * up_sum
        r["cg"][c] = slope_up
        r["cu"][c] = activated
        hid = slope_up * gate_dir + activated * up_dir
        r["h"][c, place(c)] = jnp.concatenate([hid[:, :half], hid[:, half:]], axis=0).astype(BF)
        ag_copy("h", "h", k - 1, c).start()

    def ag_step(buf, tag, l, c):
        ag_wait(buf, tag, l, c)
        ag_copy(buf, tag, l - 1, c).start()

    def down_part(c):
        ag_wait("h", "h", 0, c)
        down_copy(c).wait()
        got = r["h"][c].astype(F32)
        rows = [jnp.concatenate([got[p, :tpo], got[p, tpo:]], axis=1) for p in range(n)]
        hid = jnp.concatenate(rows, axis=0).astype(BF)
        r["acc"][...] += jnp.dot(hid, dn[c], preferred_element_type=F32)

    def run(lags, stages):
        def step(i, carry):
            for lag, stage in zip(lags, stages):
                c = i - lag

                @pl.when(jnp.logical_and(c >= 0, c < CHUNKS))
                def _():
                    stage(c)
            return carry

        lax.fori_loop(0, CHUNKS + lags[-1], step, 0)

    run(
        [0, 1] + [1 + 2 * l for l in range(1, k)] + [2 * k - 1 + l for l in range(1, k + 1)],
        [project]
        + [functools.partial(rs_step, "h", l) for l in range(k - 1)]
        + [hidden]
        + [functools.partial(ag_step, "h", "h", l) for l in range(k - 1, 0, -1)]
        + [down_part],
    )

    acc, q, qs, o = r["acc"], r["q"], r["qs"], r["o"]

    def part_send(d):
        return row_copy(qs.at[d], q.at[d], "p", d)

    def out_send(d):
        return row_copy(o.at[rows_of(row)], o.at[rows_of(row)], "o", d)

    def out_arrival(d):
        return row_copy(o.at[rows_of(source(d))], o.at[rows_of(source(d))], "o", d)

    for d in range(1, nr):
        qs[d] = acc[rows_of(peer(d))].astype(BF)
        part_send(d).start()
    out = acc[rows_of(row)]
    for d in range(1, nr):
        part_send(d).wait()
        out = out + q[d].astype(F32)
    o[rows_of(row)] = (out * scale).astype(BF)
    for d in range(1, nr):
        out_send(d).start()
    r["tt"][...] = jnp.transpose(x[...].astype(F32)).astype(BF)
    for d in range(1, nr):
        out_send(d).wait_send()
        out_arrival(d).wait_recv()

    starts = [sum(len(g) for g in GROUPS[:i]) for i in range(len(GROUPS))]

    def held(g):
        return pl.ds(starts[g], len(GROUPS[g]))

    def back_copy(l, g):
        c = GROUPS[g][0]
        return pltpu.make_async_remote_copy(
            src_ref=r["bs%d" % l].at[held(g)],
            dst_ref=r["br%d" % l].at[held(g)],
            send_sem=r["bss"].at[l, g],
            recv_sem=r["brs"].at[l, g],
            device_id=(row, partner(l, c)),
            device_id_type=MESH,
        )

    def cot_copy(l, g, arriving=False):
        c = GROUPS[g][0]
        size = 1 << (k - 1 - l)
        base = lax.div(place(c), size) * size
        if arriving:
            base = base + (1 - 2 * bit(l, c)) * size
        part = r["g"].at[held(g), pl.ds(base, size)]
        return pltpu.make_async_remote_copy(
            src_ref=part,
            dst_ref=part,
            send_sem=r["bsa"].at[l, g],
            recv_sem=r["bra"].at[l, g],
            device_id=(row, partner(l, c)),
            device_id_type=MESH,
        )

    def cot_wait(l, g):
        cot_copy(l, g).wait_send()
        cot_copy(l, g, arriving=True).wait_recv()

    def back(g):
        pb = r["pb"]
        b = bit(0, 0)
        span = total // 2
        for i, c in enumerate(GROUPS[g]):
            at = starts[g] + i
            pb[i] = lax.dot_general(
                o[...], dn[c], (((1,), (1,)), ((), ())), preferred_element_type=F32
            )
            for p in range(n // 2):
                rows = pl.ds(pl.multiple_of((1 - b) * span + p * tpo, tpo), tpo)
                both = [pb[i, rows, :half], pb[i, rows, half:]]
                r["bs0"][at, p] = jnp.concatenate(both, axis=0).astype(BF)
        back_copy(0, g).start()
        for i, c in enumerate(GROUPS[g]):
            at = starts[g] + i
            for p in range(n // 2):
                rows = pl.ds(pl.multiple_of(b * span + p * tpo, tpo), tpo)
                both = [pb[i, rows, :half], pb[i, rows, half:]]
                r["bk0"][at, p] = jnp.concatenate(both, axis=0)

    def back_step(l, g):
        back_copy(l, g).wait()
        kept, got = r["bk%d" % l], r["br%d" % l]
        m = kept.shape[1] // 2
        b = bit(l + 1, GROUPS[g][0])
        other, mine = pl.ds((1 - b) * m, m), pl.ds(b * m, m)
        at = held(g)
        r["bs%d" % (l + 1)][at] = (kept[at, other] + got[at, other].astype(F32)).astype(BF)
        back_copy(l + 1, g).start()
        r["bk%d" % (l + 1)][at] = kept[at, mine] + got[at, mine].astype(F32)

    def cots(g):
        back_copy(k - 1, g).wait()
        for i, c in enumerate(GROUPS[g]):
            at = starts[g] + i
            sums = r["bk%d" % (k - 1)][at, 0] + r["br%d" % (k - 1)][at, 0].astype(F32)
            back_sum = jnp.concatenate([sums[:tpo], sums[tpo:]], axis=1)
            both = [back_sum * r["cg"][c], back_sum * r["cu"][c]]
            r["g"][at, place(c)] = jnp.concatenate(both, axis=0).astype(BF)
        cot_copy(k - 1, g).start()

    def cot_step(l, g):
        cot_wait(l, g)
        cot_copy(l - 1, g).start()

    def spread(g):
        cot_wait(0, g)
        for i, c in enumerate(GROUPS[g]):
            got = r["g"][starts[g] + i].astype(F32)
            r["gc"][c] = jnp.concatenate([got[p, :tpo] for p in range(n)], axis=0).astype(BF)
            r["uc"][c] = jnp.concatenate([got[p, tpo:] for p in range(n)], axis=0).astype(BF)

    stages = [back]
    stages += [functools.partial(back_step, l) for l in range(k - 1)]
    stages += [cots]
    stages += [functools.partial(cot_step, l) for l in range(k - 1, 0, -1)]
    stages += [spread]
    for i in range(len(GROUPS) + BACK_LAG * (len(stages) - 1)):
        for s, stage in enumerate(stages):
            g = i - s * BACK_LAG
            if 0 <= g < len(GROUPS):
                stage(g)


def product_kernel(tt_ref, gc_ref, uc_ref, gate_ref, up_ref):
    depth, chunk = gate_ref.shape
    for cot_ref, out_ref in ((gc_ref, gate_ref), (uc_ref, up_ref)):
        for col in range(0, chunk, 256):
            cot = cot_ref[0, :, col:col + 256]
            for at in range(0, depth, 256):
                part = jnp.dot(tt_ref[at:at + 256], cot, preferred_element_type=F32)
                out_ref[at:at + 256, col:col + 256] = part.astype(BF)


def body(n, nr, tokens, gate_weight, up_weight, down_weight, gate_tangent, up_tangent):
    k = n.bit_length() - 1
    depth, units = gate_weight.shape
    total = tokens.shape[0] * nr
    chunk = units // CHUNKS
    half = chunk // 2
    tpo = total // n
    dma = pltpu.SemaphoreType.DMA
    vm = pltpu.VMEM
    scratch = [
        ("x", vm((total, depth), BF)),
        ("w", vm((SLOTS, 4, depth, chunk), BF)),
        ("dn", vm((CHUNKS, chunk, depth), BF)),
        ("pf", vm((4, total, chunk), F32)),
        ("pb", vm((max(len(g) for g in GROUPS), total, chunk), F32)),
        ("h", vm((CHUNKS, n, 2 * tpo, half), BF)),
        ("g", vm((CHUNKS, n, 2 * tpo, chunk), BF)),
        ("cg", vm((CHUNKS, tpo, chunk), F32)),
        ("cu", vm((CHUNKS, tpo, chunk), F32)),
        ("acc", vm((total, depth), F32)),
        ("q", vm((nr, total // nr, depth), BF)),
        ("qs", vm((nr, total // nr, depth), BF)),
        ("o", vm((total, depth), BF)),
        ("wsem", dma((SLOTS, 4))),
        ("dsem", dma((CHUNKS,))),
        ("osem", dma),
    ]
    for tag, rows, cols in (("h", 4 * tpo, chunk), ("b", 2 * tpo, half)):
        for l in range(k):
            shape = (CHUNKS, n >> (l + 1), rows, cols)
            scratch += [
                (tag + "k%d" % l, vm(shape, F32)),
                (tag + "s%d" % l, vm(shape, BF)),
                (tag + "r%d" % l, vm(shape, BF)),
            ]
        scratch += [(tag + e, dma((k, CHUNKS))) for e in ("ss", "rs", "sa", "ra")]
    for tag in "tpo":
        scratch += [(tag + e, dma((nr,))) for e in "sr"]
    names = ["tokens", "gw", "uw", "gt", "ut", "dw", "gc", "uc", "tt"] + [s[0] for s in scratch]
    cot = jax.ShapeDtypeStruct((CHUNKS, total, chunk), BF)
    gate_cot, up_cot, tokens_t = pl.pallas_call(
        functools.partial(curvature_kernel, n, nr, k, names),
        out_shape=(cot, cot, jax.ShapeDtypeStruct((depth, total), BF)),
        in_specs=[pl.BlockSpec(memory_space=pl.ANY)] * 6,
        out_specs=[pl.BlockSpec(memory_space=pltpu.VMEM)] * 3,
        scratch_shapes=[s[1] for s in scratch],
        compiler_params=pltpu.CompilerParams(
            collective_id=0, has_side_effects=True, vmem_limit_bytes=60 * 1024 * 1024
        ),
        name="curvature",
    )(tokens, gate_weight, up_weight, gate_tangent, up_tangent, down_weight)
    product = jax.ShapeDtypeStruct((depth, units), BF)
    return pl.pallas_call(
        product_kernel,
        grid=(CHUNKS,),
        out_shape=(product, product),
        in_specs=[
            pl.BlockSpec((depth, total), lambda c: (0, 0)),
            pl.BlockSpec((1, total, chunk), lambda c: (c, 0, 0)),
            pl.BlockSpec((1, total, chunk), lambda c: (c, 0, 0)),
        ],
        out_specs=[pl.BlockSpec((depth, chunk), lambda c: (0, c))] * 2,
        compiler_params=pltpu.CompilerParams(vmem_limit_bytes=60 * 1024 * 1024),
        name="products",
    )(tokens_t, gate_cot, up_cot)


def solution(mesh):
    placed = (
        P("row", "col"),
        P("col", "row"),
        P("col", "row"),
        P("row", "col"),
        P("col", "row"),
        P("col", "row"),
    )
    return jax.shard_map(
        functools.partial(body, mesh.shape["col"], mesh.shape["row"]),
        mesh=mesh,
        in_specs=placed,
        out_specs=(P("col", "row"), P("col", "row")),
        check_vma=False,
    )
```
